32 devices in a mesh: rep: 2 (over x), grp: 8 (over z, y), loc: 2 (over core).
Axes of the slice: x: 2, y: 2, z: 4, core: 2. Of those that a mesh axis runs over, the one named last changes fastest.
Arguments:
- tokens: bfloat16 [4096, 3584], P(('rep', 'grp', 'loc')), parts along dimension 0, may hold values from -6 to 6
- route_groups: int32 [4096, 4], P(('rep', 'grp', 'loc')), parts along dimension 0, may hold values from 0 to 7, as said below
- route_weights: int32 [4096, 8], P(('rep', 'grp', 'loc')), parts along dimension 0, may hold values from 256 to 2040, as said below
- gate_weight: bfloat16 [16, 3584, 1024], P(('grp', 'loc')), may hold values from -0.09375 to 0.09375
- up_weight: bfloat16 [16, 3584, 1024], P(('grp', 'loc')), may hold values from -0.09375 to 0.09375
- down_weight: bfloat16 [16, 1024, 3584], P(('grp', 'loc')), may hold values from -0.1875 to 0.1875
Outputs:
- mixed: bfloat16 [4096, 3584], P(('rep', 'grp', 'loc')), parts along dimension 0
The draws below stay inside these ranges and needn't reach their ends.
There are 2 independent parts, one for each index of `rep`. The reference program is written for one: setup_inputs(seed, part) draws one part's arguments, and reference() takes and returns one part's arrays. A program takes and returns all parts, laid end to end along the dimension named above; an argument that names none is the same for every part. Nothing has to cross between parts.
Inputs may be any that keep to these rules, and one draw needn't show every extreme that they name: `route_groups`: each token names 4 distinct groups. Among the 128 tokens of one device no group is named by more than 80 tokens, and one group, the same on every device of a replica, is named by exactly 80 of them. `route_weights`: multiples of 8.
All inputs are finite; a program needn't handle non-finite values.
Results may differ from the reference program's by a relative error of at most 0.0065.
Values may be sent and summed in bfloat16 or wider, within the bound.
A program may use at most 128 MiB of HBM per device.

```python
import jax
import jax.numpy as jnp
from jax import lax

D = 3584
FF = 1024
TOP_GROUPS = 4
TOK_DEV = 128
CAP = 80
EXPERTS = 16
REPLICA_TOKENS = 2048
N_GRP = 8
N_LOC = 2


def draw_route_groups(key, part):
    key = jax.random.fold_in(key, 11)
    key_hot, key_rank, key_tok, key_col = jax.random.split(key, 4)
    blocks = N_GRP * N_LOC
    others = N_GRP - 1
    hot = jax.random.randint(key_hot, (), 0, N_GRP, dtype=jnp.int32)
    rest = TOK_DEV * TOP_GROUPS - CAP
    index_j = jnp.arange(others + 1, dtype=jnp.int32)
    weight_cum = 2 * others * index_j + index_j * (index_j - 1) // 2
    bounds = CAP + rest * weight_cum // weight_cum[others]
    rank_scores = jax.random.randint(key_rank, (blocks, others), 0, 1 << 20, dtype=jnp.int32) * others + jnp.arange(others, dtype=jnp.int32)[None, :]
    ranked = jnp.argsort(rank_scores, axis=1).astype(jnp.int32)
    other_ids = (hot + 1 + ranked) % N_GRP
    spots = jnp.arange(TOK_DEV * TOP_GROUPS, dtype=jnp.int32)
    run_index = jnp.sum((spots[:, None] >= bounds[None, 1:others]).astype(jnp.int32), axis=1)
    labels = jnp.where(spots[None, :] < CAP, hot, other_ids[:, run_index])
    table = labels.reshape(blocks, TOP_GROUPS, TOK_DEV).transpose(0, 2, 1)
    tok_scores = jax.random.randint(key_tok, (blocks, TOK_DEV), 0, 1 << 20, dtype=jnp.int32) * TOK_DEV + jnp.arange(TOK_DEV, dtype=jnp.int32)[None, :]
    tok_order = jnp.argsort(tok_scores, axis=1).astype(jnp.int32)
    table = jnp.take_along_axis(table, tok_order[:, :, None], axis=1)
    col_scores = jax.random.randint(key_col, (blocks, TOK_DEV, TOP_GROUPS), 0, 1 << 20, dtype=jnp.int32) * TOP_GROUPS + jnp.arange(TOP_GROUPS, dtype=jnp.int32)[None, None, :]
    col_order = jnp.argsort(col_scores, axis=2).astype(jnp.int32)
    table = jnp.take_along_axis(table, col_order, axis=2)
    return table.reshape(REPLICA_TOKENS, TOP_GROUPS).astype(jnp.int32)


def draw_route_weights(key, part):
    key = jax.random.fold_in(key, 23)
    value_rows = jax.random.randint(key, (REPLICA_TOKENS, TOP_GROUPS * N_LOC), 32, 256, dtype=jnp.int32)
    return (value_rows * 8).astype(jnp.int32)


def steps_of(own_key, extent, pieces, smallest, largest):
    def one(position, parts):
        draws = jax.random.uniform(jax.random.fold_in(jax.random.fold_in(own_key, 6), position), (parts,), jnp.float32, smallest / len(pieces), largest / len(pieces))
        return jnp.repeat(jnp.exp(draws), extent[position] // parts).reshape((-1,) + (1,) * (len(extent) - position - 1))

    factor_of = one(*pieces[0])
    for cut in pieces[1:]:
        factor_of = factor_of * one(*cut)
    return factor_of


def bell_draw(stream_key, dims, spread, most, cuts=(), held_as=jnp.bfloat16):
    factor_of = steps_of(stream_key, dims, cuts, -0.22, 0.18) if cuts else 1.0
    result = jax.random.normal(stream_key, dims, jnp.float32) * spread * factor_of
    return jnp.minimum(jnp.maximum(result, -most), most).astype(held_as)


def setup_inputs(seed: int = 0, part: int = 0) -> dict:
    key_list = jax.random.split(jax.random.key(seed), 7)
    part_splits = jax.random.split(jax.random.fold_in(key_list[6], part), 7)
    return {
        "tokens": bell_draw(part_splits[0], (REPLICA_TOKENS, D), 1.0, 6.0, ((0, 16),)),
        "route_groups": draw_route_groups(jax.random.fold_in(jax.random.fold_in(key_list[6], part), 71), part),
        "route_weights": draw_route_weights(jax.random.fold_in(jax.random.fold_in(key_list[6], part), 71), part),
        "gate_weight": bell_draw(key_list[3], (EXPERTS, D, FF), D ** -0.5, 0.09375, ((0, 16),)),
        "up_weight": bell_draw(key_list[4], (EXPERTS, D, FF), D ** -0.5, 0.09375, ((0, 16),)),
        "down_weight": bell_draw(key_list[5], (EXPERTS, FF, D), FF ** -0.5, 0.1875, ((0, 16),)),
    }


def reference(tokens, route_groups, route_weights, gate_weight, up_weight, down_weight):
    group_ids = jnp.arange(N_GRP, dtype=jnp.int32)
    onehot = (route_groups[:, :, None] == group_ids[None, None, :]).astype(jnp.float32)
    picked = jnp.sum(onehot, axis=1)
    scaled = route_weights.reshape(REPLICA_TOKENS, TOP_GROUPS, N_LOC).astype(jnp.float32) / 4096.0
    token_portions = jnp.einsum('tjv,tjl->vtl', onehot, scaled)
    positions = jnp.arange(REPLICA_TOKENS, dtype=jnp.int32)
    limit = N_GRP * N_LOC * CAP
    gates = gate_weight.reshape(N_GRP, N_LOC, D, FF)
    ups = up_weight.reshape(N_GRP, N_LOC, D, FF)
    downs = down_weight.reshape(N_GRP, N_LOC, FF, D)

    def one_group(total, items):
        chosen, share, gate_w, up_w, down_w = items
        keys = jnp.where(chosen > 0.5, positions, positions + REPLICA_TOKENS).astype(jnp.int32)
        order = jnp.argsort(keys)[:limit].astype(jnp.int32)
        valid = chosen[order]
        rows = tokens[order]
        part = jnp.zeros((limit, D), jnp.float32)
        for local in range(N_LOC):
            gate = jnp.dot(rows, gate_w[local], preferred_element_type=jnp.float32)
            upper = jnp.dot(rows, up_w[local], preferred_element_type=jnp.float32)
            hidden = (jax.nn.silu(gate) * upper).astype(jnp.bfloat16)
            out = jnp.dot(hidden, down_w[local], preferred_element_type=jnp.float32)
            weighted = lax.optimization_barrier((share[order, local][:, None] * out).astype(jnp.bfloat16))
            part = part + weighted.astype(jnp.float32)
        rounded = lax.optimization_barrier(part.astype(jnp.bfloat16))
        part = rounded.astype(jnp.float32) * valid[:, None]
        return total.at[order].add(part), None

    total = jnp.zeros((REPLICA_TOKENS, D), jnp.float32)
    total, unused = lax.scan(one_group, total, (picked.T, token_portions, gates, ups, downs))
    return total.astype(jnp.bfloat16)
```

```python
import jax
import jax.numpy as jnp
from jax import lax
from jax.sharding import PartitionSpec as P


def shards(tokens, route_groups, route_weights, gate_weight, up_weight, down_weight):
    n_rows, width = tokens.shape
    n_group = lax.axis_size("grp")
    n_loc = lax.axis_size("loc")
    top_groups = route_groups.shape[1]
    capacity = n_rows * top_groups * 5 // (n_group * 4)
    n_src = n_group * n_loc
    axes = ("grp", "loc")

    routing = jnp.concatenate([route_groups, route_weights], axis=1)
    routing = lax.all_gather(routing, axes, axis=0, tiled=False)
    everyone = lax.all_gather(tokens, axes, axis=0, tiled=False)

    group = lax.axis_index("grp")
    local = lax.axis_index("loc")
    hit = routing[:, :, :top_groups] == group
    weights = routing[:, :, top_groups:].reshape(n_src, n_rows, top_groups, n_loc)
    mine = jnp.sum(
        jnp.where(jnp.arange(n_loc, dtype=jnp.int32) == local, weights, 0), axis=3
    )
    share = jnp.sum(jnp.where(hit, mine, 0), axis=2).astype(jnp.float32) / 4096.0
    picked = jnp.any(hit, axis=2).astype(jnp.int32)
    slots = jnp.cumsum(picked, axis=1) - picked
    assign = (picked[:, None, :] == 1) & (
        slots[:, None, :] == jnp.arange(capacity, dtype=jnp.int32)[None, :, None]
    )
    slot_share = jnp.sum(jnp.where(assign, share[:, None, :], 0.0), axis=2)
    place = assign.astype(jnp.bfloat16)
    rows = jnp.einsum(
        "sqt,std->sqd", place, everyone, preferred_element_type=jnp.float32
    ).astype(jnp.bfloat16).reshape(n_src * capacity, width)
    gate = jnp.dot(rows, gate_weight[0], preferred_element_type=jnp.float32)
    upper = jnp.dot(rows, up_weight[0], preferred_element_type=jnp.float32)
    hidden = (jax.nn.silu(gate) * upper).astype(jnp.bfloat16)
    results = jnp.dot(hidden, down_weight[0], preferred_element_type=jnp.float32)
    weighted = (results.reshape(n_src, capacity, width) * slot_share[..., None]).astype(jnp.bfloat16)
    partial = jnp.einsum(
        "sqt,sqd->std", place, weighted, preferred_element_type=jnp.float32
    ).astype(jnp.bfloat16)
    return lax.psum_scatter(
        partial.reshape(n_src * n_rows, width), axes, scatter_dimension=0, tiled=True
    )


def solution(mesh):
    return jax.shard_map(
        shards,
        mesh=mesh,
        in_specs=(
            P(("rep", "grp", "loc"), None),
            P(("rep", "grp", "loc"), None),
            P(("rep", "grp", "loc"), None),
            P(("grp", "loc"), None, None),
            P(("grp", "loc"), None, None),
            P(("grp", "loc"), None, None),
        ),
        out_specs=P(("rep", "grp", "loc"), None),
        check_vma=False,
    )
```

```python
import jax
import jax.numpy as jnp
from jax import lax
from jax.experimental import pallas as pl
from jax.experimental.pallas import tpu as pltpu
from jax.sharding import PartitionSpec as P

MESH = pl.DeviceIdType.MESH
LANES = 128


def flip(bit, other):
    return bit + other - 2 * bit * other


def fused_kernel(
    own, gate_hbm, up_hbm, down_hbm, out_ref,
    tok, gate_w, up_w, down_w, hidden, keep, lsend, lrecv, yrecv, zrecv,
    w_sem, own_sem,
    zg_s, zg_r, yg_s, yg_r, lg_s, lg_r, lr_s, lr_r, yr_s, yr_r, zr_s, zr_r,
):
    n_rows, width = out_ref.shape
    ff = hidden.shape[1]
    steps = keep.shape[0]
    grp = lax.axis_index("grp")
    loc = lax.axis_index("loc")
    y = grp % 2
    zb = (grp // 2) % 2
    za = grp // 4

    def at_z(dz):
        return {"grp": 4 * flip(za, dz // 2) + 2 * flip(zb, dz % 2) + y, "loc": loc}

    y_peer = {"grp": grp + 1 - 2 * y, "loc": loc}
    l_peer = {"grp": grp, "loc": 1 - loc}

    def remote(src, dst, send, recv, peer):
        return pltpu.make_async_remote_copy(
            src_ref=src, dst_ref=dst, send_sem=send, recv_sem=recv,
            device_id=peer, device_id_type=MESH,
        )

    def z_gather(dz):
        return remote(own, tok.at[2 * dz, 0], zg_s.at[dz], zg_r.at[dz], at_z(dz))

    def y_gather(dz, src=None):
        src = tok.at[2 * dz, 0] if src is None else src
        return remote(src, tok.at[2 * dz + 1, 0], yg_s.at[dz], yg_r.at[dz], y_peer)

    def l_gather(s, src=None):
        src = tok.at[s, 0] if src is None else src
        return remote(src, tok.at[s, 1], lg_s.at[s], lg_r.at[s], l_peer)

    def l_reduce(s):
        return remote(lsend.at[s % 2], lrecv.at[s], lr_s.at[s], lr_r.at[s], l_peer)

    def y_reduce(dz):
        return remote(keep.at[2 * dz + 1], yrecv.at[dz], yr_s.at[dz], yr_r.at[dz], y_peer)

    def z_reduce(dz):
        return remote(keep.at[2 * dz], zrecv.at[dz], zr_s.at[dz], zr_r.at[dz], at_z(dz))

    barrier = pltpu.get_barrier_semaphore()
    peers = [at_z(1), at_z(2), at_z(3), y_peer, l_peer]
    for peer in peers:
        pl.semaphore_signal(barrier, inc=1, device_id=peer, device_id_type=MESH)
    w_copies = [
        pltpu.make_async_copy(gate_hbm.at[0], gate_w, w_sem.at[0]),
        pltpu.make_async_copy(up_hbm.at[0], up_w, w_sem.at[1]),
        pltpu.make_async_copy(down_hbm.at[0], down_w, w_sem.at[2]),
    ]
    own_copy = pltpu.make_async_copy(own, tok.at[0, 0], own_sem)
    own_copy.start()
    pl.semaphore_wait(barrier, len(peers))
    l_gather(0, own).start()
    y_gather(0, own).start()
    for dz in (1, 2, 3):
        z_gather(dz).start()
    for copy in w_copies:
        copy.start()
    own_copy.wait()
    for copy in w_copies:
        copy.wait()

    part = 16

    def add_core_peer(s):
        l_reduce(s).wait_recv()

        @pl.loop(0, n_rows // part)
        def _(r):
            rows = pl.ds(pl.multiple_of(r * part, part), part)
            keep[s, rows, :] = (
                keep[s, rows, :].astype(jnp.float32) + lrecv[s, rows, :].astype(jnp.float32)
            ).astype(jnp.bfloat16)

        @pl.when(s % 2 == 1)
        def _():
            y_reduce(s // 2).start()

    def add_y_peer(dz):
        y_reduce(dz).wait_recv()

        @pl.loop(0, n_rows // part)
        def _(r):
            rows = pl.ds(pl.multiple_of(r * part, part), part)
            keep[2 * dz, rows, :] = (
                keep[2 * dz, rows, :].astype(jnp.float32) + yrecv[dz, rows, :].astype(jnp.float32)
            ).astype(jnp.bfloat16)

        z_reduce(dz).start()

    expert = 2 * grp + loc
    tile = 256
    span = 512

    @pl.loop(0, steps)
    def _(s):
        dz = s // 2

        @pl.when(jnp.logical_and(s % 2 == 0, s > 0))
        def _():
            z_gather(dz).wait_recv()
            y_gather(dz).start()

        @pl.when(s % 2 == 1)
        def _():
            y_gather(dz).wait_recv()

        @pl.when(s > 0)
        def _():
            l_gather(s).start()
            add_core_peer(s - 1)

        @pl.when(s == steps - 1)
        def _():
            add_y_peer(1)

        l_gather(s).wait_recv()

        @pl.when(s > 1)
        def _():
            l_reduce(s - 2).wait_send()

        extra = tok[s, :, :, width:].reshape(2 * n_rows, LANES).astype(jnp.float32)
        lane = lax.broadcasted_iota(jnp.int32, (2 * n_rows, LANES), 1)
        share = jnp.sum(jnp.where(lane == expert, extra, 0.0), axis=1, keepdims=True)

        @pl.loop(0, ff // tile)
        def _(c):
            cols = pl.ds(pl.multiple_of(c * tile, tile), tile)
            x = tok[s, :, :, :width].reshape(2 * n_rows, width)
            gate = jnp.dot(x, gate_w[:, cols], preferred_element_type=jnp.float32)
            upper = jnp.dot(x, up_w[:, cols], preferred_element_type=jnp.float32)
            act = gate / (1.0 + jnp.exp(-gate)) * upper
            hidden[:, cols] = act.astype(jnp.bfloat16)

        @pl.loop(0, width // span)
        def _(c):
            cols = pl.ds(pl.multiple_of(c * span, span), span)
            res = jnp.dot(hidden[...], down_w[:, cols], preferred_element_type=jnp.float32)
            res = (res * share).astype(jnp.bfloat16)
            keep[s, :, cols] = res[:n_rows]
            lsend[s % 2, :, cols] = res[n_rows:]

        l_reduce(s).start()

    add_core_peer(steps - 1)
    add_y_peer(2)
    add_y_peer(3)
    y_reduce(0).wait_recv()
    for dz in (1, 2, 3):
        z_reduce(dz).wait_recv()

    @pl.loop(0, n_rows // part)
    def _(r):
        rows = pl.ds(pl.multiple_of(r * part, part), part)
        total = keep[0, rows, :].astype(jnp.float32) + yrecv[0, rows, :].astype(jnp.float32)
        for dz in (1, 2, 3):
            total = total + zrecv[dz, rows, :].astype(jnp.float32)
        out_ref[rows, :] = total.astype(jnp.bfloat16)

    for dz in (1, 2, 3):
        z_gather(dz).wait_send()
        z_reduce(dz).wait_send()
    for dz in range(4):
        y_gather(dz, own if dz == 0 else None).wait_send()
        y_reduce(dz).wait_send()
    for s in range(steps):
        l_gather(s, own if s == 0 else None).wait_send()
    for s in (steps - 2, steps - 1):
        l_reduce(s).wait_send()


def fused_shards(tokens, route_groups, route_weights, gate_weight, up_weight, down_weight):
    n_rows, width = tokens.shape
    n_group = lax.axis_size("grp")
    n_loc = lax.axis_size("loc")
    top_groups = route_groups.shape[1]
    ff = gate_weight.shape[2]
    lane = jnp.arange(LANES, dtype=jnp.int32)
    weights = route_weights.reshape(n_rows, top_groups, n_loc)
    named = route_groups[:, :, None] * n_loc + jnp.arange(n_loc, dtype=jnp.int32)
    shares = jnp.sum(
        jnp.where(named[..., None] == lane, weights[..., None], 0), axis=(1, 2)
    ).astype(jnp.float32) / 4096.0
    wide = jnp.concatenate([tokens, shares.astype(jnp.bfloat16)], axis=1)
    full = width + LANES
    bf16 = jnp.bfloat16
    dma = pltpu.SemaphoreType.DMA
    return pl.pallas_call(
        fused_kernel,
        out_shape=jax.ShapeDtypeStruct((n_rows, width), bf16),
        in_specs=[pl.BlockSpec(memory_space=pl.ANY)] * 4,
        out_specs=pl.BlockSpec(memory_space=pltpu.VMEM),
        scratch_shapes=[
            pltpu.VMEM((n_group, 2, n_rows, full), bf16),
            pltpu.VMEM((width, ff), bf16),
            pltpu.VMEM((width, ff), bf16),
            pltpu.VMEM((ff, width), bf16),
            pltpu.VMEM((2 * n_rows, ff), bf16),
            pltpu.VMEM((n_group, n_rows, width), bf16),
            pltpu.VMEM((2, n_rows, width), bf16),
            pltpu.VMEM((n_group, n_rows, width), bf16),
            pltpu.VMEM((4, n_rows, width), bf16),
            pltpu.VMEM((4, n_rows, width), bf16),
            dma((3,)), dma,
            dma((4,)), dma((4,)), dma((4,)), dma((4,)),
            dma((8,)), dma((8,)), dma((8,)), dma((8,)),
            dma((4,)), dma((4,)), dma((4,)), dma((4,)),
        ],
        compiler_params=pltpu.CompilerParams(
            collective_id=0, has_side_effects=True, vmem_limit_bytes=65011712
        ),
        cost_estimate=pl.CostEstimate(
            flops=6 * n_group * n_loc * n_rows * width * ff,
            bytes_accessed=6 * width * ff,
            transcendentals=n_group * n_loc * n_rows * ff,
        ),
    )(wide, gate_weight, up_weight, down_weight)


def shards(tokens, route_groups, route_weights, gate_weight, up_weight, down_weight):
    n_rows, width = tokens.shape
    n_group = lax.axis_size("grp")
    n_loc = lax.axis_size("loc")
    top_groups = route_groups.shape[1]
    capacity = n_rows * top_groups * 5 // (n_group * 4)
    n_src = n_group * n_loc
    axes = ("grp", "loc")

    routing = jnp.concatenate([route_groups, route_weights], axis=1)
    routing = lax.all_gather(routing, axes, axis=0, tiled=False)
    everyone = lax.all_gather(tokens, axes, axis=0, tiled=False)

    group = lax.axis_index("grp")
    local = lax.axis_index("loc")
    hit = routing[:, :, :top_groups] == group
    weights = routing[:, :, top_groups:].reshape(n_src, n_rows, top_groups, n_loc)
    mine = jnp.sum(
        jnp.where(jnp.arange(n_loc, dtype=jnp.int32) == local, weights, 0), axis=3
    )
    share = jnp.sum(jnp.where(hit, mine, 0), axis=2).astype(jnp.float32) / 4096.0
    picked = jnp.any(hit, axis=2).astype(jnp.int32)
    slots = jnp.cumsum(picked, axis=1) - picked
    assign = (picked[:, None, :] == 1) & (
        slots[:, None, :] == jnp.arange(capacity, dtype=jnp.int32)[None, :, None]
    )
    slot_share = jnp.sum(jnp.where(assign, share[:, None, :], 0.0), axis=2)
    place = assign.astype(jnp.bfloat16)
    rows = jnp.einsum(
        "sqt,std->sqd", place, everyone, preferred_element_type=jnp.float32
    ).astype(jnp.bfloat16).reshape(n_src * capacity, width)
    gate = jnp.dot(rows, gate_weight[0], preferred_element_type=jnp.float32)
    upper = jnp.dot(rows, up_weight[0], preferred_element_type=jnp.float32)
    hidden = (jax.nn.silu(gate) * upper).astype(jnp.bfloat16)
    results = jnp.dot(hidden, down_weight[0], preferred_element_type=jnp.float32)
    weighted = (results.reshape(n_src, capacity, width) * slot_share[..., None]).astype(jnp.bfloat16)
    partial = jnp.einsum(
        "sqt,sqd->std", place, weighted, preferred_element_type=jnp.float32
    ).astype(jnp.bfloat16)
    return lax.psum_scatter(
        partial.reshape(n_src * n_rows, width), axes, scatter_dimension=0, tiled=True
    )


def solution(mesh):
    fits = mesh.shape["grp"] == 8 and mesh.shape["loc"] == 2
    return jax.shard_map(
        fused_shards if fits else shards,
        mesh=mesh,
        in_specs=(
            P(("rep", "grp", "loc"), None),
            P(("rep", "grp", "loc"), None),
            P(("rep", "grp", "loc"), None),
            P(("grp", "loc"), None, None),
            P(("grp", "loc"), None, None),
            P(("grp", "loc"), None, None),
        ),
        out_specs=P(("rep", "grp", "loc"), None),
        check_vma=False,
    )
```

```python
import jax
import jax.numpy as jnp
from jax import lax
from jax.experimental import pallas as pl
from jax.experimental.pallas import tpu as pltpu
from jax.sharding import PartitionSpec as P

MESH = pl.DeviceIdType.MESH
LANES = 128


def fused_kernel(
    own, gate_hbm, up_hbm, down_hbm, out_ref,
    tok_a, tok_b, picked, gate_w, up_w, down_w, hidden,
    keep_a, keep_b, lsend_a, lsend_b, lrecv_a, lrecv_b, yrecv, zrecv,
    w_sem, own_sem, zg_s, zg_r, yg_s, yg_r, la_s, la_r, lb_s, lb_r,
    ra_s, ra_r, rb_s, rb_r, yr_s, yr_r, zr_s, zr_r,
):
    n_rows, width = out_ref.shape
    cap = picked.shape[1]
    ff = hidden.shape[1]
    n_z = keep_a.shape[0]
    bf16 = jnp.bfloat16
    grp = lax.axis_index("grp")
    loc = lax.axis_index("loc")
    y = grp % 2
    z = grp // 2
    y_grp = grp + 1 - 2 * y
    expert = 2 * grp + loc
    tile = 256
    span = 512
    part = 16

    def at_z(zs):
        return {"grp": 2 * zs + y, "loc": loc}

    y_peer = {"grp": y_grp, "loc": loc}
    l_peer = {"grp": grp, "loc": 1 - loc}

    def remote(src, dst, send, recv, peer):
        return pltpu.make_async_remote_copy(
            src_ref=src, dst_ref=dst, send_sem=send, recv_sem=recv,
            device_id=peer, device_id_type=MESH,
        )

    def z_gather(zs, up):
        block = tok_a.at[zs, 0]
        return remote(block, block, zg_s.at[zs, up], zg_r.at[zs], at_z(z + 2 * up - 1))

    def z_arrival(zs):
        block = tok_a.at[zs, 0]
        return remote(block, block, zg_s.at[zs, 0], zg_r.at[zs], at_z(zs))

    def y_gather(zs):
        return remote(picked.at[zs], tok_b.at[zs, 0], yg_s.at[zs], yg_r.at[zs], y_peer)

    def l_gather_a(zs):
        return remote(tok_a.at[zs, 0], tok_a.at[zs, 1], la_s.at[zs], la_r.at[zs], l_peer)

    def l_gather_b(zs):
        return remote(tok_b.at[zs, 0], tok_b.at[zs, 1], lb_s.at[zs], lb_r.at[zs], l_peer)

    def l_reduce_a(zs):
        return remote(lsend_a, lrecv_a.at[zs], ra_s.at[zs], ra_r.at[zs], l_peer)

    def l_reduce_b(zs):
        return remote(lsend_b, lrecv_b.at[zs], rb_s.at[zs], rb_r.at[zs], l_peer)

    def y_reduce(zs):
        return remote(keep_b.at[zs], yrecv.at[zs], yr_s.at[zs], yr_r.at[zs], y_peer)

    def z_reduce(zs, slot):
        return remote(keep_a.at[zs], zrecv.at[slot], zr_s.at[zs], zr_r.at[slot], at_z(zs))

    def order(k):
        m = (z % 2) * (1 - z // 2) + (1 - z % 2) * (z // 2)
        v = k + m * (1 - k // 2) * (1 - 2 * k)
        return v + (z // 2) * (3 - 2 * v)

    def column(extra, lane_index):
        lane = lax.broadcasted_iota(jnp.int32, extra.shape, 1)
        return jnp.sum(
            jnp.where(lane == lane_index, extra.astype(jnp.float32), 0.0), axis=1, keepdims=True
        )

    def placer(zs, lanes):
        slot = column(tok_a[zs, 0, :, width:], LANES // 2 + y_grp)
        lane = lax.broadcasted_iota(jnp.int32, (n_rows, lanes), 1).astype(jnp.float32)
        return jnp.where(slot == lane + 1.0, 1.0, 0.0)

    def pick(zs):
        place = placer(zs, n_rows).T.astype(bf16)[:cap]

        def some(cols):
            picked[zs, :, cols] = jnp.dot(
                place, tok_a[zs, 0, :, cols], preferred_element_type=jnp.float32
            ).astype(bf16)

        @pl.loop(0, width // span)
        def _(c):
            some(pl.ds(pl.multiple_of(c * span, span), span))

        some(pl.ds(width, LANES))

    def run_expert(tok, zs, keep, lsend):
        rows = tok.shape[2]
        share = column(tok[zs, :, :, width:].reshape(2 * rows, LANES), expert)

        @pl.loop(0, ff // tile)
        def _(c):
            cols = pl.ds(pl.multiple_of(c * tile, tile), tile)
            x = tok[zs, :, :, :width].reshape(2 * rows, width)
            gate = jnp.dot(x, gate_w[:, cols], preferred_element_type=jnp.float32)
            upper = jnp.dot(x, up_w[:, cols], preferred_element_type=jnp.float32)
            act = gate / (1.0 + jnp.exp(-gate)) * upper
            hidden[: 2 * rows, cols] = act.astype(bf16)

        @pl.loop(0, width // span)
        def _(c):
            cols = pl.ds(pl.multiple_of(c * span, span), span)
            res = jnp.dot(
                hidden[: 2 * rows, :], down_w[:, cols], preferred_element_type=jnp.float32
            )
            res = (res * share).astype(bf16)
            keep[zs, :, cols] = res[:rows]
            lsend[:, cols] = res[rows:]

    def add_core_peer(keep, lrecv, zs):
        @pl.loop(0, keep.shape[1] // part)
        def _(r):
            rows = pl.ds(pl.multiple_of(r * part, part), part)
            keep[zs, rows, :] = (
                keep[zs, rows, :].astype(jnp.float32) + lrecv[zs, rows, :].astype(jnp.float32)
            ).astype(bf16)

    def add_y_peer(zs):
        y_reduce(zs).wait_recv()
        place = placer(zs, cap).astype(bf16)

        @pl.loop(0, width // span)
        def _(c):
            cols = pl.ds(pl.multiple_of(c * span, span), span)
            spread = jnp.dot(place, yrecv[zs, :, cols], preferred_element_type=jnp.float32)
            keep_a[zs, :, cols] = (keep_a[zs, :, cols].astype(jnp.float32) + spread).astype(bf16)

    barrier = pltpu.get_barrier_semaphore()
    peers = [at_z((z + j) % n_z) for j in range(1, n_z)] + [y_peer, l_peer]
    own_copy = pltpu.make_async_copy(own, tok_a.at[z, 0], own_sem)
    own_copy.start()
    for peer in peers:
        pl.semaphore_signal(barrier, inc=1, device_id=peer, device_id_type=MESH)
    w_copies = [
        pltpu.make_async_copy(gate_hbm.at[0], gate_w, w_sem.at[0]),
        pltpu.make_async_copy(up_hbm.at[0], up_w, w_sem.at[1]),
        pltpu.make_async_copy(down_hbm.at[0], down_w, w_sem.at[2]),
    ]
    own_copy.wait()
    for copy in w_copies:
        copy.start()
    pl.semaphore_wait(barrier, len(peers))

    @pl.loop(0, n_z + 1)
    def _(k):
        zs = order(k)
        zp = order(k - 1)

        @pl.when(k < n_z)
        def _():
            @pl.when(k > 0)
            def _():
                z_arrival(zs).wait_recv()

            @pl.when(jnp.logical_and(zs <= z, z < n_z - 1))
            def _():
                z_gather(zs, 1).start()

            @pl.when(jnp.logical_and(zs >= z, z > 0))
            def _():
                z_gather(zs, 0).start()

            l_gather_a(zs).start()
            pick(zs)
            y_gather(zs).start()

        @pl.when(k == 0)
        def _():
            for copy in w_copies:
                copy.wait()

        @pl.when(k > 0)
        def _():
            y_gather(zp).wait_recv()
            l_gather_b(zp).start()

        @pl.when(k < n_z)
        def _():
            l_gather_a(zs).wait_recv()

            @pl.when(k > 0)
            def _():
                l_reduce_a(zp).wait_send()

            run_expert(tok_a, zs, keep_a, lsend_a)
            l_reduce_a(zs).start()

        @pl.when(k > 0)
        def _():
            l_gather_b(zp).wait_recv()

            @pl.when(k > 1)
            def _():
                l_reduce_b(order(k - 2)).wait_send()

            run_expert(tok_b, zp, keep_b, lsend_b)
            l_reduce_b(zp).start()

        @pl.when(k < n_z)
        def _():
            l_reduce_a(zs).wait_recv()
            add_core_peer(keep_a, lrecv_a, zs)

        @pl.when(k > 0)
        def _():
            l_reduce_b(zp).wait_recv()
            add_core_peer(keep_b, lrecv_b, zp)
            y_reduce(zp).start()

        @pl.when(k > 1)
        def _():
            add_y_peer(order(k - 2))

        @pl.when(k > 2)
        def _():
            z_reduce(order(k - 2), z).start()

    last = order(n_z - 1)
    add_y_peer(last)
    z_reduce(last, z).start()
    others = [(z + j) % n_z for j in range(1, n_z)]
    for zs in others:
        z_reduce(zs, zs).wait_recv()

    @pl.loop(0, n_rows // part)
    def _(r):
        rows = pl.ds(pl.multiple_of(r * part, part), part)
        total = keep_a[z, rows, :].astype(jnp.float32)
        for zs in others:
            total = total + zrecv[zs, rows, :].astype(jnp.float32)
        out_ref[rows, :] = total.astype(bf16)

    for zs in others:
        z_reduce(zs, z).wait_send()
    l_reduce_a(last).wait_send()
    l_reduce_b(last).wait_send()

    @pl.loop(0, n_z)
    def _(zs):
        @pl.when(jnp.logical_and(zs <= z, z < n_z - 1))
        def _():
            z_gather(zs, 1).wait_send()

        @pl.when(jnp.logical_and(zs >= z, z > 0))
        def _():
            z_gather(zs, 0).wait_send()

        y_gather(zs).wait_send()
        y_reduce(zs).wait_send()
        l_gather_a(zs).wait_send()
        l_gather_b(zs).wait_send()


def fused_shards(tokens, route_groups, route_weights, gate_weight, up_weight, down_weight):
    n_rows, width = tokens.shape
    n_group = lax.axis_size("grp")
    n_loc = lax.axis_size("loc")
    top_groups = route_groups.shape[1]
    cap = n_rows * top_groups * 5 // (n_group * 4)
    ff = gate_weight.shape[2]
    half = LANES // 2
    lane = jnp.arange(half, dtype=jnp.int32)
    weights = route_weights.reshape(n_rows, top_groups, n_loc)
    named = route_groups[:, :, None] * n_loc + jnp.arange(n_loc, dtype=jnp.int32)
    shares = jnp.sum(
        jnp.where(named[..., None] == lane, weights[..., None], 0), axis=(1, 2)
    ).astype(jnp.float32) / 4096.0
    chosen = jnp.any(route_groups[:, :, None] == lane, axis=1)
    slots = jnp.where(chosen, jnp.cumsum(chosen.astype(jnp.int32), axis=0), 0)
    bf16 = jnp.bfloat16
    wide = jnp.concatenate([tokens, shares.astype(bf16), slots.astype(bf16)], axis=1)
    full = width + LANES
    n_z = n_group // 2
    vmem = pltpu.VMEM
    dma = pltpu.SemaphoreType.DMA
    return pl.pallas_call(
        fused_kernel,
        out_shape=jax.ShapeDtypeStruct((n_rows, width), bf16),
        in_specs=[pl.BlockSpec(memory_space=pl.ANY)] * 4,
        out_specs=pl.BlockSpec(memory_space=pltpu.VMEM),
        scratch_shapes=[
            vmem((n_z, 2, n_rows, full), bf16),
            vmem((n_z, 2, cap, full), bf16),
            vmem((n_z, cap, full), bf16),
            vmem((width, ff), bf16),
            vmem((width, ff), bf16),
            vmem((ff, width), bf16),
            vmem((2 * n_rows, ff), bf16),
            vmem((n_z, n_rows, width), bf16),
            vmem((n_z, cap, width), bf16),
            vmem((n_rows, width), bf16),
            vmem((cap, width), bf16),
            vmem((n_z, n_rows, width), bf16),
            vmem((n_z, cap, width), bf16),
            vmem((n_z, cap, width), bf16),
            vmem((n_z, n_rows, width), bf16),
            dma((3,)), dma, dma((n_z, 2)), dma((n_z,)),
        ] + [dma((n_z,))] * 14,
        compiler_params=pltpu.CompilerParams(
            collective_id=0, has_side_effects=True, vmem_limit_bytes=65011712
        ),
        cost_estimate=pl.CostEstimate(
            flops=6 * n_group * (n_rows + cap) * width * ff,
            bytes_accessed=6 * width * ff,
            transcendentals=n_group * (n_rows + cap) * ff,
        ),
    )(wide, gate_weight, up_weight, down_weight)


def shards(tokens, route_groups, route_weights, gate_weight, up_weight, down_weight):
    n_rows, width = tokens.shape
    n_group = lax.axis_size("grp")
    n_loc = lax.axis_size("loc")
    top_groups = route_groups.shape[1]
    capacity = n_rows * top_groups * 5 // (n_group * 4)
    n_src = n_group * n_loc
    axes = ("grp", "loc")

    routing = jnp.concatenate([route_groups, route_weights], axis=1)
    routing = lax.all_gather(routing, axes, axis=0, tiled=False)
    everyone = lax.all_gather(tokens, axes, axis=0, tiled=False)

    group = lax.axis_index("grp")
    local = lax.axis_index("loc")
    hit = routing[:, :, :top_groups] == group
    weights = routing[:, :, top_groups:].reshape(n_src, n_rows, top_groups, n_loc)
    mine = jnp.sum(
        jnp.where(jnp.arange(n_loc, dtype=jnp.int32) == local, weights, 0), axis=3
    )
    share = jnp.sum(jnp.where(hit, mine, 0), axis=2).astype(jnp.float32) / 4096.0
    picked = jnp.any(hit, axis=2).astype(jnp.int32)
    slots = jnp.cumsum(picked, axis=1) - picked
    assign = (picked[:, None, :] == 1) & (
        slots[:, None, :] == jnp.arange(capacity, dtype=jnp.int32)[None, :, None]
    )
    slot_share = jnp.sum(jnp.where(assign, share[:, None, :], 0.0), axis=2)
    place = assign.astype(jnp.bfloat16)
    rows = jnp.einsum(
        "sqt,std->sqd", place, everyone, preferred_element_type=jnp.float32
    ).astype(jnp.bfloat16).reshape(n_src * capacity, width)
    gate = jnp.dot(rows, gate_weight[0], preferred_element_type=jnp.float32)
    upper = jnp.dot(rows, up_weight[0], preferred_element_type=jnp.float32)
    hidden = (jax.nn.silu(gate) * upper).astype(jnp.bfloat16)
    results = jnp.dot(hidden, down_weight[0], preferred_element_type=jnp.float32)
    weighted = (results.reshape(n_src, capacity, width) * slot_share[..., None]).astype(jnp.bfloat16)
    partial = jnp.einsum(
        "sqt,sqd->std", place, weighted, preferred_element_type=jnp.float32
    ).astype(jnp.bfloat16)
    return lax.psum_scatter(
        partial.reshape(n_src * n_rows, width), axes, scatter_dimension=0, tiled=True
    )


def solution(mesh):
    fits = mesh.shape["grp"] == 8 and mesh.shape["loc"] == 2
    return jax.shard_map(
        fused_shards if fits else shards,
        mesh=mesh,
        in_specs=(
            P(("rep", "grp", "loc"), None),
            P(("rep", "grp", "loc"), None),
            P(("rep", "grp", "loc"), None),
            P(("grp", "loc"), None, None),
            P(("grp", "loc"), None, None),
            P(("grp", "loc"), None, None),
        ),
        out_specs=P(("rep", "grp", "loc"), None),
        check_vma=False,
    )
```

```python
import jax
import jax.numpy as jnp
from jax import lax
from jax.experimental import pallas as pl
from jax.experimental.pallas import tpu as pltpu
from jax.sharding import PartitionSpec as P

MESH = pl.DeviceIdType.MESH
LANES = 128


def fused_kernel(
    own, gate_hbm, up_hbm, down_hbm, out_ref,
    tok_a, tok_b, picked, gate_w, up_w, down_w, hidden,
    keep_a, keep_b, lsend_a, lsend_b, lrecv_a, lrecv_b, yrecv, zrecv,
    w_sem, own_sem, zg_s, zg_r, yg_s, yg_r, la_s, la_r, lb_s, lb_r,
    ra_s, ra_r, rb_s, rb_r, yr_s, yr_r, zr_s, zr_r,
):
    n_rows, width = out_ref.shape
    cap = picked.shape[1]
    ff = hidden.shape[1]
    n_z = keep_a.shape[0]
    bf16 = jnp.bfloat16
    grp = lax.axis_index("grp")
    loc = lax.axis_index("loc")
    y = grp % 2
    z = grp // 2
    y_grp = grp + 1 - 2 * y
    inner = (z % 2) * (1 - z // 2) + (1 - z % 2) * (z // 2)
    expert = 2 * grp + loc
    tile = 256
    span = 512
    part = 16

    def at_z(zs):
        return {"grp": 2 * zs + y, "loc": loc}

    y_peer = {"grp": y_grp, "loc": loc}
    l_peer = {"grp": grp, "loc": 1 - loc}

    def remote(src, dst, send, recv, peer):
        return pltpu.make_async_remote_copy(
            src_ref=src, dst_ref=dst, send_sem=send, recv_sem=recv,
            device_id=peer, device_id_type=MESH,
        )

    def z_gather(zs, up):
        block = tok_a.at[zs, 0]
        return remote(block, block, zg_s.at[zs, up], zg_r.at[zs], at_z(z + 2 * up - 1))

    def z_arrival(zs):
        block = tok_a.at[zs, 0]
        return remote(block, block, zg_s.at[zs, 0], zg_r.at[zs], at_z(zs))

    def y_gather(zs):
        return remote(picked.at[zs], tok_b.at[zs, 0], yg_s.at[zs], yg_r.at[zs], y_peer)

    def l_gather_a(zs):
        return remote(tok_a.at[zs, 0], tok_a.at[zs, 1], la_s.at[zs], la_r.at[zs], l_peer)

    def l_gather_b(zs):
        return remote(tok_b.at[zs, 0], tok_b.at[zs, 1], lb_s.at[zs], lb_r.at[zs], l_peer)

    def l_reduce_a(zs):
        return remote(lsend_a, lrecv_a.at[zs], ra_s.at[zs], ra_r.at[zs], l_peer)

    def l_reduce_b(zs):
        return remote(lsend_b, lrecv_b.at[zs], rb_s.at[zs], rb_r.at[zs], l_peer)

    def y_reduce(zs):
        return remote(keep_b.at[zs], yrecv.at[zs], yr_s.at[zs], yr_r.at[zs], y_peer)

    def z_reduce(zs, slot):
        return remote(keep_a.at[zs], zrecv.at[slot], zr_s.at[zs], zr_r.at[slot], at_z(zs))

    def order(k):
        v = k + inner * (1 - k // 3) * (1 - 3 * (k // 2))
        return v + (z // 2) * (3 - 2 * v)

    def column(extra, lane_index):
        lane = lax.broadcasted_iota(jnp.int32, extra.shape, 1)
        return jnp.sum(
            jnp.where(lane == lane_index, extra.astype(jnp.float32), 0.0), axis=1, keepdims=True
        )

    def placer(zs, lanes):
        slot = column(tok_a[zs, 0, :, width:], LANES // 2 + y_grp)
        lane = lax.broadcasted_iota(jnp.int32, (n_rows, lanes), 1).astype(jnp.float32)
        return jnp.where(slot == lane + 1.0, 1.0, 0.0)

    def pick(zs):
        place = placer(zs, n_rows).T.astype(bf16)[:cap]

        def some(cols):
            picked[zs, :, cols] = jnp.dot(
                place, tok_a[zs, 0, :, cols], preferred_element_type=jnp.float32
            ).astype(bf16)

        @pl.loop(0, width // span)
        def _(c):
            some(pl.ds(pl.multiple_of(c * span, span), span))

        some(pl.ds(width, LANES))

    def run_expert(tok, zs, keep, lsend):
        rows = tok.shape[2]
        share = column(tok[zs, :, :, width:].reshape(2 * rows, LANES), expert)

        @pl.loop(0, ff // tile)
        def _(c):
            cols = pl.ds(pl.multiple_of(c * tile, tile), tile)
            x = tok[zs, :, :, :width].reshape(2 * rows, width)
            gate = jnp.dot(x, gate_w[:, cols], preferred_element_type=jnp.float32)
            upper = jnp.dot(x, up_w[:, cols], preferred_element_type=jnp.float32)
            act = gate / (1.0 + jnp.exp(-gate)) * upper
            hidden[: 2 * rows, cols] = act.astype(bf16)

        @pl.loop(0, width // span)
        def _(c):
            cols = pl.ds(pl.multiple_of(c * span, span), span)
            res = jnp.dot(
                hidden[: 2 * rows, :], down_w[:, cols], preferred_element_type=jnp.float32
            )
            res = (res * share).astype(bf16)
            keep[zs, :, cols] = res[:rows]
            lsend[:, cols] = res[rows:]

    def add_core_peer(keep, lrecv, zs):
        @pl.loop(0, keep.shape[1] // part)
        def _(r):
            rows = pl.ds(pl.multiple_of(r * part, part), part)
            keep[zs, rows, :] = (
                keep[zs, rows, :].astype(jnp.float32) + lrecv[zs, rows, :].astype(jnp.float32)
            ).astype(bf16)

    def add_y_peer(zs):
        y_reduce(zs).wait_recv()
        place = placer(zs, cap).astype(bf16)

        @pl.loop(0, width // span)
        def _(c):
            cols = pl.ds(pl.multiple_of(c * span, span), span)
            spread = jnp.dot(place, yrecv[zs, :, cols], preferred_element_type=jnp.float32)
            keep_a[zs, :, cols] = (keep_a[zs, :, cols].astype(jnp.float32) + spread).astype(bf16)

    barrier = pltpu.get_barrier_semaphore()
    peers = [at_z((z + j) % n_z) for j in range(1, n_z)] + [y_peer, l_peer]
    own_copy = pltpu.make_async_copy(own, tok_a.at[z, 0], own_sem)
    own_copy.start()
    for peer in peers:
        pl.semaphore_signal(barrier, inc=1, device_id=peer, device_id_type=MESH)
    w_copies = [
        pltpu.make_async_copy(gate_hbm.at[0], gate_w, w_sem.at[0]),
        pltpu.make_async_copy(up_hbm.at[0], up_w, w_sem.at[1]),
        pltpu.make_async_copy(down_hbm.at[0], down_w, w_sem.at[2]),
    ]
    own_copy.wait()
    for copy in w_copies:
        copy.start()
    pl.semaphore_wait(barrier, len(peers))

    def pass_on(zs, arrives):
        @pl.when(arrives)
        def _():
            z_arrival(zs).wait_recv()

        @pl.when(jnp.logical_and(zs <= z, z < n_z - 1))
        def _():
            z_gather(zs, 1).start()

        @pl.when(jnp.logical_and(zs >= z, z > 0))
        def _():
            z_gather(zs, 0).start()

    @pl.loop(0, n_z + 1)
    def _(k):
        zs = order(k)
        zp = order(k - 1)

        @pl.when(k < n_z)
        def _():
            @pl.when(jnp.logical_or(k != 2, inner == 0))
            def _():
                pass_on(zs, k > 0)

            @pl.when(jnp.logical_and(k == 1, inner == 1))
            def _():
                pass_on(order(2), True)

            l_gather_a(zs).start()
            pick(zs)
            y_gather(zs).start()

        @pl.when(k == 0)
        def _():
            for copy in w_copies:
                copy.wait()

        @pl.when(k > 0)
        def _():
            y_gather(zp).wait_recv()
            l_gather_b(zp).start()

        @pl.when(k < n_z)
        def _():
            l_gather_a(zs).wait_recv()

            @pl.when(k > 0)
            def _():
                l_reduce_a(zp).wait_send()

            run_expert(tok_a, zs, keep_a, lsend_a)
            l_reduce_a(zs).start()

        @pl.when(k > 0)
        def _():
            l_gather_b(zp).wait_recv()

            @pl.when(k > 1)
            def _():
                l_reduce_b(order(k - 2)).wait_send()

            run_expert(tok_b, zp, keep_b, lsend_b)
            l_reduce_b(zp).start()

        @pl.when(k < n_z)
        def _():
            l_reduce_a(zs).wait_recv()
            add_core_peer(keep_a, lrecv_a, zs)

        @pl.when(k > 0)
        def _():
            l_reduce_b(zp).wait_recv()
            add_core_peer(keep_b, lrecv_b, zp)
            y_reduce(zp).start()

        @pl.when(k > 1)
        def _():
            add_y_peer(order(k - 2))

        @pl.when(k > 2)
        def _():
            z_reduce(order(k - 2), z).start()

    last = order(n_z - 1)
    add_y_peer(last)
    z_reduce(last, z).start()
    others = [(z + j) % n_z for j in range(1, n_z)]
    for zs in others:
        z_reduce(zs, zs).wait_recv()

    @pl.loop(0, n_rows // part)
    def _(r):
        rows = pl.ds(pl.multiple_of(r * part, part), part)
        total = keep_a[z, rows, :].astype(jnp.float32)
        for zs in others:
            total = total + zrecv[zs, rows, :].astype(jnp.float32)
        out_ref[rows, :] = total.astype(bf16)

    for zs in others:
        z_reduce(zs, z).wait_send()
    l_reduce_a(last).wait_send()
    l_reduce_b(last).wait_send()

    @pl.loop(0, n_z)
    def _(zs):
        @pl.when(jnp.logical_and(zs <= z, z < n_z - 1))
        def _():
            z_gather(zs, 1).wait_send()

        @pl.when(jnp.logical_and(zs >= z, z > 0))
        def _():
            z_gather(zs, 0).wait_send()

        y_gather(zs).wait_send()
        y_reduce(zs).wait_send()
        l_gather_a(zs).wait_send()
        l_gather_b(zs).wait_send()


def fused_shards(tokens, route_groups, route_weights, gate_weight, up_weight, down_weight):
    n_rows, width = tokens.shape
    n_group = lax.axis_size("grp")
    n_loc = lax.axis_size("loc")
    top_groups = route_groups.shape[1]
    cap = n_rows * top_groups * 5 // (n_group * 4)
    ff = gate_weight.shape[2]
    half = LANES // 2
    lane = jnp.arange(half, dtype=jnp.int32)
    weights = route_weights.reshape(n_rows, top_groups, n_loc)
    named = route_groups[:, :, None] * n_loc + jnp.arange(n_loc, dtype=jnp.int32)
    shares = jnp.sum(
        jnp.where(named[..., None] == lane, weights[..., None], 0), axis=(1, 2)
    ).astype(jnp.float32) / 4096.0
    chosen = jnp.any(route_groups[:, :, None] == lane, axis=1)
    slots = jnp.where(chosen, jnp.cumsum(chosen.astype(jnp.int32), axis=0), 0)
    bf16 = jnp.bfloat16
    wide = jnp.concatenate([tokens, shares.astype(bf16), slots.astype(bf16)], axis=1)
    full = width + LANES
    n_z = n_group // 2
    vmem = pltpu.VMEM
    dma = pltpu.SemaphoreType.DMA
    return pl.pallas_call(
        fused_kernel,
        out_shape=jax.ShapeDtypeStruct((n_rows, width), bf16),
        in_specs=[pl.BlockSpec(memory_space=pl.ANY)] * 4,
        out_specs=pl.BlockSpec(memory_space=pltpu.VMEM),
        scratch_shapes=[
            vmem((n_z, 2, n_rows, full), bf16),
            vmem((n_z, 2, cap, full), bf16),
            vmem((n_z, cap, full), bf16),
            vmem((width, ff), bf16),
            vmem((width, ff), bf16),
            vmem((ff, width), bf16),
            vmem((2 * n_rows, ff), bf16),
            vmem((n_z, n_rows, width), bf16),
            vmem((n_z, cap, width), bf16),
            vmem((n_rows, width), bf16),
            vmem((cap, width), bf16),
            vmem((n_z, n_rows, width), bf16),
            vmem((n_z, cap, width), bf16),
            vmem((n_z, cap, width), bf16),
            vmem((n_z, n_rows, width), bf16),
            dma((3,)), dma, dma((n_z, 2)), dma((n_z,)),
        ] + [dma((n_z,))] * 14,
        compiler_params=pltpu.CompilerParams(
            collective_id=0, has_side_effects=True, vmem_limit_bytes=65011712
        ),
        cost_estimate=pl.CostEstimate(
            flops=6 * n_group * (n_rows + cap) * width * ff,
            bytes_accessed=6 * width * ff,
            transcendentals=n_group * (n_rows + cap) * ff,
        ),
    )(wide, gate_weight, up_weight, down_weight)


def shards(tokens, route_groups, route_weights, gate_weight, up_weight, down_weight):
    n_rows, width = tokens.shape
    n_group = lax.axis_size("grp")
    n_loc = lax.axis_size("loc")
    top_groups = route_groups.shape[1]
    capacity = n_rows * top_groups * 5 // (n_group * 4)
    n_src = n_group * n_loc
    axes = ("grp", "loc")

    routing = jnp.concatenate([route_groups, route_weights], axis=1)
    routing = lax.all_gather(routing, axes, axis=0, tiled=False)
    everyone = lax.all_gather(tokens, axes, axis=0, tiled=False)

    group = lax.axis_index("grp")
    local = lax.axis_index("loc")
    hit = routing[:, :, :top_groups] == group
    weights = routing[:, :, top_groups:].reshape(n_src, n_rows, top_groups, n_loc)
    mine = jnp.sum(
        jnp.where(jnp.arange(n_loc, dtype=jnp.int32) == local, weights, 0), axis=3
    )
    share = jnp.sum(jnp.where(hit, mine, 0), axis=2).astype(jnp.float32) / 4096.0
    picked = jnp.any(hit, axis=2).astype(jnp.int32)
    slots = jnp.cumsum(picked, axis=1) - picked
    assign = (picked[:, None, :] == 1) & (
        slots[:, None, :] == jnp.arange(capacity, dtype=jnp.int32)[None, :, None]
    )
    slot_share = jnp.sum(jnp.where(assign, share[:, None, :], 0.0), axis=2)
    place = assign.astype(jnp.bfloat16)
    rows = jnp.einsum(
        "sqt,std->sqd", place, everyone, preferred_element_type=jnp.float32
    ).astype(jnp.bfloat16).reshape(n_src * capacity, width)
    gate = jnp.dot(rows, gate_weight[0], preferred_element_type=jnp.float32)
    upper = jnp.dot(rows, up_weight[0], preferred_element_type=jnp.float32)
    hidden = (jax.nn.silu(gate) * upper).astype(jnp.bfloat16)
    results = jnp.dot(hidden, down_weight[0], preferred_element_type=jnp.float32)
    weighted = (results.reshape(n_src, capacity, width) * slot_share[..., None]).astype(jnp.bfloat16)
    partial = jnp.einsum(
        "sqt,sqd->std", place, weighted, preferred_element_type=jnp.float32
    ).astype(jnp.bfloat16)
    return lax.psum_scatter(
        partial.reshape(n_src * n_rows, width), axes, scatter_dimension=0, tiled=True
    )


def solution(mesh):
    fits = mesh.shape["grp"] == 8 and mesh.shape["loc"] == 2
    return jax.shard_map(
        fused_shards if fits else shards,
        mesh=mesh,
        in_specs=(
            P(("rep", "grp", "loc"), None),
            P(("rep", "grp", "loc"), None),
            P(("rep", "grp", "loc"), None),
            P(("grp", "loc"), None, None),
            P(("grp", "loc"), None, None),
            P(("grp", "loc"), None, None),
        ),
        out_specs=P(("rep", "grp", "loc"), None),
        check_vma=False,
    )
```
